512 devices in a mesh: blk: 128 (over x, z, y_hi), feat: 4 (over y_lo, core).
Axes of the slice: x: 4, y: 4 (y_hi: 2, y_lo: 2; y = y_hi * 2 + y_lo), z: 16, core: 2. Of those that a mesh axis runs over, the one named last changes fastest.
Arguments:
- hidden_query: bfloat16 [65536, 4096], P('blk', 'feat'), may hold values from -6 to 6
- hidden_passage: bfloat16 [16384, 4096], P('blk', 'feat'), may hold values from -6 to 6
- embed_gain: float32 [4096], P('feat'), may hold values from 0.5 to 1.5
- positive: int32 [65536], P('blk'), may hold values from 0 to 16383, as said below
- tail_count: int32 [65536], P('blk'), may hold values from 769 to 896, as said below
Outputs:
- grad_query: float32 [65536, 4096], P('blk', 'feat')
- grad_passage: float32 [16384, 4096], P('blk', 'feat')
- grad_gain: float32 [4096], P('feat')
- loss: float32 [65536], P('blk')
The draws below stay inside these ranges and needn't reach their ends.
Inputs may be any that keep to these rules, and one draw needn't show every extreme that they name: positive[q] lies in block q // 512 of the passages: from (q // 512) * 128 to (q // 512) * 128 + 127. Some query takes each end of the range of tail_count.
All inputs are finite; a program needn't handle non-finite values.
Results may differ from the reference program's by a relative error of at most 0.0041.
Values may be sent and summed in bfloat16 or wider, within the bound.
A program may use at most 64 MiB of HBM per device.

```python
import jax
import jax.numpy as jnp
from jax import lax

D = 4096
QB = 512
PB = 128
REACH = 3
QUERIES = 65536
PASSAGES = 16384
N_BLK = 128


def draw_positive(key, part):
    key = jax.random.fold_in(key, 11)
    owner = jnp.arange(QUERIES, dtype=jnp.int32) // QB
    inside = jax.random.randint(key, (QUERIES,), 0, PB, dtype=jnp.int32)
    return (owner * PB + inside).astype(jnp.int32)


def draw_tail_count(key, part):
    key = jax.random.fold_in(key, 23)
    widest = 2 * REACH + 1
    lowest = (widest - 1) * PB + 1
    counts = jax.random.randint(key, (QUERIES,), lowest, widest * PB + 1, dtype=jnp.int32)
    counts = counts.at[0].set(widest * PB)
    counts = counts.at[1].set(lowest)
    return counts.astype(jnp.int32)


def levels(own_key, dims, split, least, largest):
    factor_of = 1.0
    for position, parts in split:
        steps = jax.random.uniform(jax.random.fold_in(jax.random.fold_in(own_key, 6), position), (parts,), jnp.float32, least / len(split), largest / len(split))
        factor_of = factor_of * jnp.repeat(jnp.exp(steps), dims[position] // parts).reshape((-1,) + (1,) * (len(dims) - 1 - position))
    return factor_of


def centred(rng, extent, scale, limit, split=(), held_as=jnp.bfloat16):
    result = jax.random.normal(rng, extent, jnp.float32) * scale
    if len(split) > 0:
        result = levels(rng, extent, split, -0.22, 0.18) * result
    return jnp.clip(result, min=-limit, max=limit).astype(held_as)


def setup_inputs(seed: int = 0) -> dict:
    keys = jax.random.split(jax.random.key(seed), 6)
    return {
        "hidden_query": centred(keys[0], (QUERIES, D), 1.0, 6.0, ((0, 128), (1, 4))),
        "hidden_passage": centred(keys[1], (PASSAGES, D), 1.0, 6.0, ((0, 128), (1, 4))),
        "embed_gain": jnp.clip(1.0 + 0.1 * jax.random.normal(keys[2], (D,), jnp.float32), 0.5, 1.5),
        "positive": draw_positive(jax.random.fold_in(keys[5], 71), 0),
        "tail_count": draw_tail_count(jax.random.fold_in(keys[5], 71), 0),
    }


margin = 1.0
loss_scale = 128.0


def reference(hidden_query, hidden_passage, embed_gain, positive, tail_count):
    queries = (hidden_query.astype(jnp.float32) * embed_gain).astype(jnp.bfloat16)
    passages = (hidden_passage.astype(jnp.float32) * embed_gain).astype(jnp.bfloat16)
    score_scale = D ** -0.5
    offsets = jnp.arange(-REACH, REACH + 1, dtype=jnp.int32)
    inside = jnp.arange(PB, dtype=jnp.int32)
    signed = jnp.repeat(offsets, PB)
    order = 2 * jnp.abs(signed) - jnp.where(signed > 0, 1, 0).astype(jnp.int32)
    rank = (order * PB + jnp.tile(inside, 2 * REACH + 1)).astype(jnp.int32)

    def one_block(acc, block):
        col_blocks = (block + offsets) % N_BLK
        column = (col_blocks[:, None] * PB + inside[None, :]).reshape(-1).astype(jnp.int32)
        window = passages[column]
        start = (block * QB).astype(jnp.int32)
        query_rows = lax.dynamic_slice_in_dim(queries, start, QB, 0)
        pos_rows = lax.dynamic_slice_in_dim(positive, start, QB, 0)
        count_rows = lax.dynamic_slice_in_dim(tail_count, start, QB, 0)
        scores = jnp.dot(query_rows, window.T, preferred_element_type=jnp.float32) * score_scale
        pos_hot = column[None, :] == pos_rows[:, None]
        weights = jnp.where((rank[None, :] < count_rows[:, None]) & jnp.logical_not(pos_hot), 1.0, 0.0).astype(jnp.float32)
        anchor = jnp.sum(jnp.where(pos_hot, scores, 0.0), axis=1)
        excess = scores - anchor[:, None] + margin
        counts = count_rows.astype(jnp.float32)
        loss = jnp.sum(weights * jax.nn.softplus(excess), axis=1) / counts
        grads = loss_scale * weights * jax.nn.sigmoid(excess) / counts[:, None]
        row_total = jnp.sum(grads, axis=1)
        gmat = (grads - jnp.where(pos_hot, row_total[:, None], 0.0)).astype(jnp.bfloat16)
        dquery = jnp.dot(gmat, window, preferred_element_type=jnp.float32) * score_scale
        dpart = jnp.dot(gmat.T, query_rows, preferred_element_type=jnp.float32) * score_scale
        return acc.at[column].add(dpart), (dquery, loss)

    start_acc = jnp.zeros((PASSAGES, D), jnp.float32)
    dpassage, (dquery, loss) = lax.scan(one_block, start_acc, jnp.arange(N_BLK, dtype=jnp.int32))
    dquery = dquery.reshape(QUERIES, D)
    loss = loss.reshape(QUERIES)
    grad_gain = jnp.sum(dquery * hidden_query.astype(jnp.float32), axis=0) + jnp.sum(dpassage * hidden_passage.astype(jnp.float32), axis=0)
    return dquery * embed_gain, dpassage * embed_gain, grad_gain, loss
```

```python
import jax
import jax.numpy as jnp
from jax import lax
from jax.experimental import pallas as pl
from jax.experimental.pallas import tpu as pltpu
from jax.sharding import PartitionSpec as P

MESH = pl.DeviceIdType.MESH
MARGIN = 1.0
LOSS_SCALE = 128.0
D = 4096
SCALE = D ** (-0.5)
N_BLK = 128
NZ = 16
NXY = 8
PB = 128
QB = 512
HALF = 256
WIDTH = 1024

OWN, R, F, K, FR, KR, FAR = range(7)
OFFSET = {OWN: 0, R: 1, F: 2, K: -2, FR: 3, KR: -1, FAR: -3}
ROLES = (R, F, K, FR, KR, FAR)

ORDER = (
    "S0", "r0", "H0", "r1", "S1", "S2", "H1", "S3", "H2", "H3", "k0", "G1", "G2", "k1", "S5", "G3",
    "D2", "D3", "S4", "H5", "H4", "D1", "S6", "G5", "G4", "H6", "D5", "D4", "G6", "G0",
    "D6", "D0", "Q", "N", "M", "Z", "X",
)
FC = 2
RC = 4
CHAIN = True


def kernel(
    hq_hbm, hp_hbm, gain_hbm, pos_hbm, tail_hbm,
    gq_hbm, gp_hbm, gg_ref, loss_ref,
    hq, gain_ref, pos_ref, tail_ref, hpt, q, p, sx, rx, hb, hr, gt, rpart, kpart, ret_out, ret_in, dq, dp, zbuf, xbuf, lbuf,
    local_sem, out_sem, fwd_send, fwd_recv, x1_send, x1_recv, x2_send, x2_recv,
    x3_send, x3_recv, ret_send, ret_recv, z_send, z_recv, xy_send, xy_recv, loss_send, loss_recv,
):
    b = lax.axis_index("blk")
    f = lax.axis_index("feat")
    h = lax.rem(b, 2)
    x = b // 32
    z = lax.rem(b, 32) // 2
    core = lax.rem(f, 2)
    sigma = 1 - 2 * h

    def block_at(role):
        return lax.rem(b + N_BLK + sigma * OFFSET[role], N_BLK)

    def dev(role):
        return (block_at(role), f)

    mate = (b, f + 1 - 2 * core)
    across = (b, lax.rem(f + 2, 4))

    def z_peer(k):
        return (x * 32 + lax.rem(z + k, NZ) * 2 + h, f)

    place = x * 2 + h

    def xy_peer(k):
        e = lax.rem(place + k, NXY)
        return ((e // 2) * 32 + z * 2 + lax.rem(e, 2), f)

    load_hp = pltpu.make_async_copy(hp_hbm, hpt.at[OWN], local_sem.at[0])
    load_hq = pltpu.make_async_copy(hq_hbm, hq, local_sem.at[1])
    small = [
        pltpu.make_async_copy(src, dst, local_sem.at[2 + i])
        for i, (src, dst) in enumerate(
            ((gain_hbm, gain_ref), (pos_hbm, pos_ref), (tail_hbm, tail_ref))
        )
    ]
    for copy in [load_hp, load_hq] + small:
        copy.start()

    peers = [dev(r) for r in ROLES] + [mate, across]
    peers += [z_peer(k) for k in range(1, NZ)] + [xy_peer(k) for k in range(1, NXY)]
    barrier = pltpu.get_barrier_semaphore()
    for peer in peers:
        pl.semaphore_signal(barrier, inc=1, device_id=peer, device_id_type=MESH)
    pl.semaphore_wait(barrier, len(peers))

    sends = []

    def send(src, dst, s_sem, r_sem, to):
        copy = pltpu.make_async_remote_copy(
            src_ref=src, dst_ref=dst, send_sem=s_sem, recv_sem=r_sem,
            device_id=to, device_id_type=MESH,
        )
        copy.start()
        sends.append(copy)
        return copy

    def forward(src, slot, i, to):
        rows = pl.ds(i * (PB // FC), PB // FC)
        return send(
            src.at[rows, :], hpt.at[slot, rows, :], fwd_send.at[slot, i], fwd_recv.at[slot, i], dev(to)
        )

    fwd = {}
    for i in range(FC):
        fwd[R, i] = forward(hp_hbm, R, i, R)
    for i in range(FC):
        fwd[K, i] = forward(hp_hbm, K, i, F)
        fwd[F, i] = forward(hp_hbm, F, i, K)

    for copy in small:
        copy.wait()
    gain = gain_ref[...]
    pos_rows = [pos_ref[pl.ds(i, 1), :] for i in range(4)]
    pos_all = jnp.concatenate(pos_rows, axis=1) - b * PB
    pos_half = (
        jnp.concatenate([pos_ref[pl.ds(2 * core, 1), :], pos_ref[pl.ds(2 * core + 1, 1), :]], axis=1)
        - b * PB
    )
    tail_half = jnp.concatenate(
        [tail_ref[pl.ds(2 * core, 1), :], tail_ref[pl.ds(2 * core + 1, 1), :]], axis=1
    )
    count_half = tail_half.astype(jnp.float32)
    col_half = lax.broadcasted_iota(jnp.int32, (PB, HALF), 0)

    x1, x2, x3, ret = {}, {}, {}, {}
    state = {"anchor": None, "loss": 0.0, "total": 0.0, "gain": 0.0}

    load_hq.wait()
    q[...] = (hq[...].astype(jnp.float32) * gain).astype(jnp.bfloat16)
    load_hp.wait()

    def relay_r(i):
        fwd[R, i].wait_recv()
        fwd[KR, i] = forward(hpt.at[R], KR, i, F)
        fwd[FR, i] = forward(hpt.at[R], FR, i, K)

    def relay_k(i):
        fwd[KR, i].wait_recv()
        fwd[FAR, i] = forward(hpt.at[KR], FAR, i, F)

    def stage_s(t):
        if t in (F, K, FR, FAR):
            for i in range(FC):
                fwd[t, i].wait_recv()
        rows = pl.ds(t * PB, PB)
        tile = (hpt[t].astype(jnp.float32) * gain).astype(jnp.bfloat16)
        p[rows, :] = tile
        s = lax.dot_general(
            tile, q[...], (((1,), (1,)), ((), ())), preferred_element_type=jnp.float32
        ) * SCALE
        if t == OWN:
            hot = lax.broadcasted_iota(jnp.int32, (PB, QB), 0) == pos_all
            state["anchor"] = jnp.sum(jnp.where(hot, s, 0.0), axis=0, keepdims=True)
        s = s - state["anchor"]
        sx[t, 0] = s[:, :HALF]
        sx[t, 1] = s[:, HALF:]
        x1[t] = send(sx.at[t, 1 - core], rx.at[t], x1_send.at[t], x1_recv.at[t], mate)

    def stage_h(t):
        x1[t].wait_recv()
        hb[t] = (sx[t, core] + rx[t]).astype(jnp.bfloat16)
        x2[t] = send(hb.at[t], hr.at[t], x2_send.at[t], x2_recv.at[t], across)

    def stage_g(t):
        x2[t].wait_recv()
        excess = hb[t].astype(jnp.float32) + hr[t].astype(jnp.float32) + MARGIN
        signed = sigma * OFFSET[t]
        order = 2 * abs(OFFSET[t]) - jnp.where(signed > 0, 1, 0)
        live = order * PB + col_half < tail_half
        if t == OWN:
            hot = col_half == pos_half
            live = live & jnp.logical_not(hot)
        e = jnp.exp(-jnp.abs(excess))
        soft = jnp.maximum(excess, 0.0) + jnp.log1p(e)
        sig = jnp.where(excess >= 0.0, 1.0, e) / (1.0 + e)
        state["loss"] += jnp.sum(jnp.where(live, soft, 0.0), axis=0, keepdims=True)
        g = jnp.where(live, sig * (LOSS_SCALE / count_half), 0.0)
        state["total"] += jnp.sum(g, axis=0, keepdims=True)
        if t == OWN:
            g = g - jnp.where(hot, state["total"], 0.0)
            lbuf[core] = jnp.broadcast_to(state["loss"] / count_half, (8, HALF))
            state["lossx"] = send(
                lbuf.at[core], lbuf.at[core], loss_send.at[0], loss_recv.at[0], mate
            )
        rows = pl.ds(t * PB, PB)
        gt[core, rows, :] = g.astype(jnp.bfloat16)
        x3[t] = send(
            gt.at[core, rows, :], gt.at[core, rows, :], x3_send.at[t], x3_recv.at[t], mate
        )

    def give_rows(t, value, to, rows, i):
        slot = t - 1
        ret_out[slot, rows, :] = value.astype(jnp.bfloat16)
        ret[t, i] = send(
            ret_out.at[slot, rows, :], ret_in.at[slot, rows, :],
            ret_send.at[slot, i], ret_recv.at[slot, i], dev(to),
        )

    def give(t, value, to, chunks):
        n = PB // chunks
        for i in range(chunks):
            give_rows(t, value[i * n:(i + 1) * n], to, pl.ds(i * n, n), i)

    def chain_n():
        n = PB // RC
        for i in range(RC):
            rows = pl.ds(i * n, n)
            ret[FAR, i].wait_recv()
            value = kpart[rows, :] + ret_in[FAR - 1, rows, :].astype(jnp.float32)
            give_rows(KR, value, K, rows, i)

    def chain_m():
        n = PB // RC
        ret[FR, 0].wait_recv()
        for i in range(RC):
            rows = pl.ds(i * n, n)
            ret[KR, i].wait_recv()
            value = rpart[rows, :] + ret_in[FR - 1, rows, :].astype(jnp.float32)
            value = value + ret_in[KR - 1, rows, :].astype(jnp.float32)
            give_rows(R, value, R, rows, i)

    def stage_d(t):
        x3[t].wait_recv()
        rows = pl.ds(t * PB, PB)
        part = jnp.dot(gt[0, rows, :], q[:HALF, :], preferred_element_type=jnp.float32)
        part = part + jnp.dot(gt[1, rows, :], q[HALF:, :], preferred_element_type=jnp.float32)
        part = part * SCALE
        if t == OWN:
            dp[...] = part
        elif t == R:
            rpart[...] = part
        elif t == KR and CHAIN:
            kpart[...] = part
        elif t == FAR:
            give(t, part, K if CHAIN else FAR, RC)
        elif t == KR:
            give(t, part, K, RC)
        else:
            give(t, part, F if t in (F, FR) else K, 1)
        prod = part * hpt[t].astype(jnp.float32)
        state["gain"] += jnp.sum(prod.reshape(PB // 8, 8, WIDTH), axis=0)

    out_copies = []

    def stage_q():
        for i in range(2):
            rows = pl.ds(i * HALF, HALF)
            dquery = lax.dot_general(
                gt[i], p[...], (((0,), (0,)), ((), ())), preferred_element_type=jnp.float32
            ) * SCALE
            dq[rows, :] = dquery * gain
            copy = pltpu.make_async_copy(dq.at[rows, :], gq_hbm.at[rows, :], out_sem.at[i])
            copy.start()
            out_copies.append(copy)
            prod = dquery * hq[rows, :].astype(jnp.float32)
            state["gain"] += jnp.sum(prod.reshape(HALF // 8, 8, WIDTH), axis=0)
        vec = jnp.sum(state["gain"], axis=0, keepdims=True)
        for i in range(8):
            zbuf[z, pl.ds(i, 1), :] = vec[:, i * 128:(i + 1) * 128]
        for k in range(1, NZ):
            z_copies.append(
                send(zbuf.at[z], zbuf.at[z], z_send.at[k - 1], z_recv.at[k - 1], z_peer(k))
            )

    z_copies, xy_copies = [], []

    def stage_z():
        for copy in z_copies:
            copy.wait_recv()
        line = zbuf[0]
        for i in range(1, NZ):
            line = line + zbuf[i]
        xbuf[place] = line
        for k in range(1, NXY):
            xy_copies.append(
                send(xbuf.at[place], xbuf.at[place], xy_send.at[k - 1], xy_recv.at[k - 1], xy_peer(k))
            )

    def stage_x():
        for copy in xy_copies:
            copy.wait_recv()
        plane = xbuf[0]
        for i in range(1, NXY):
            plane = plane + xbuf[i]
        gg_ref[...] = plane
        state["lossx"].wait_recv()
        loss_ref[...] = jnp.concatenate([lbuf[0, 0:1, :], lbuf[1, 0:1, :]], axis=1)

    stages = {
        "S": stage_s, "H": stage_h, "G": stage_g, "D": stage_d, "r": relay_r, "k": relay_k,
        "Q": stage_q, "Z": stage_z, "X": stage_x, "N": chain_n, "M": chain_m,
    }
    for step in ORDER:
        if step == "N" and not CHAIN:
            continue
        stages[step[0]](*[int(c) for c in step[1:]])

    total = dp[...]
    for t in (F, K, R) if CHAIN else (F, K, R, FAR):
        for i in range(1 if t in (F, K) else RC):
            ret[t, i].wait_recv()
        total = total + ret_in[t - 1].astype(jnp.float32)
    dp[...] = total * gain
    copy = pltpu.make_async_copy(dp, gp_hbm, out_sem.at[2])
    copy.start()
    out_copies.append(copy)
    for copy in sends:
        copy.wait_send()
    for copy in out_copies:
        copy.wait()


def shards(hidden_query, hidden_passage, embed_gain, positive, tail_count):
    vmem = pl.BlockSpec(memory_space=pltpu.VMEM)
    hbm = pl.BlockSpec(memory_space=pl.ANY)
    dma = pltpu.SemaphoreType.DMA
    gq, gp, gg, loss = pl.pallas_call(
        kernel,
        name="retrieval",
        out_shape=(
            jax.ShapeDtypeStruct((QB, WIDTH), jnp.float32),
            jax.ShapeDtypeStruct((PB, WIDTH), jnp.float32),
            jax.ShapeDtypeStruct((8, 128), jnp.float32),
            jax.ShapeDtypeStruct((1, QB), jnp.float32),
        ),
        in_specs=[hbm] * 5,
        out_specs=(hbm, hbm, vmem, vmem),
        scratch_shapes=[
            pltpu.VMEM((QB, WIDTH), jnp.bfloat16),
            pltpu.VMEM((1, WIDTH), jnp.float32),
            pltpu.VMEM((4, 128), jnp.int32),
            pltpu.VMEM((4, 128), jnp.int32),
            pltpu.VMEM((7, PB, WIDTH), jnp.bfloat16),
            pltpu.VMEM((QB, WIDTH), jnp.bfloat16),
            pltpu.VMEM((7 * PB, WIDTH), jnp.bfloat16),
            pltpu.VMEM((7, 2, PB, HALF), jnp.float32),
            pltpu.VMEM((7, PB, HALF), jnp.float32),
            pltpu.VMEM((7, PB, HALF), jnp.bfloat16),
            pltpu.VMEM((7, PB, HALF), jnp.bfloat16),
            pltpu.VMEM((2, 7 * PB, HALF), jnp.bfloat16),
            pltpu.VMEM((PB, WIDTH), jnp.float32),
            pltpu.VMEM((PB, WIDTH), jnp.float32),
            pltpu.VMEM((6, PB, WIDTH), jnp.bfloat16),
            pltpu.VMEM((6, PB, WIDTH), jnp.bfloat16),
            pltpu.VMEM((QB, WIDTH), jnp.float32),
            pltpu.VMEM((PB, WIDTH), jnp.float32),
            pltpu.VMEM((NZ, 8, 128), jnp.float32),
            pltpu.VMEM((NXY, 8, 128), jnp.float32),
            pltpu.VMEM((2, 8, HALF), jnp.float32),
            dma((5,)), dma((3,)), dma((7, FC)), dma((7, FC)), dma((7,)), dma((7,)), dma((7,)), dma((7,)),
            dma((7,)), dma((7,)), dma((6, RC)), dma((6, RC)), dma((NZ - 1,)), dma((NZ - 1,)),
            dma((NXY - 1,)), dma((NXY - 1,)), dma((1,)), dma((1,)),
        ],
        compiler_params=pltpu.CompilerParams(
            collective_id=0, has_side_effects=True, vmem_limit_bytes=60 * 1024 * 1024
        ),
    )(
        hidden_query, hidden_passage, embed_gain.reshape(1, WIDTH),
        positive.reshape(4, 128), tail_count.reshape(4, 128),
    )
    return gq, gp, gg.reshape(WIDTH), loss.reshape(QB)


def solution(mesh):
    in_specs = (P("blk", "feat"), P("blk", "feat"), P("feat"), P("blk"), P("blk"))
    out_specs = (P("blk", "feat"), P("blk", "feat"), P("feat"), P("blk"))
    return jax.shard_map(shards, mesh=mesh, in_specs=in_specs, out_specs=out_specs, check_vma=False)
```

```python
import jax
import jax.numpy as jnp
from jax import lax
from jax.experimental import pallas as pl
from jax.experimental.pallas import tpu as pltpu
from jax.sharding import PartitionSpec as P

MESH = pl.DeviceIdType.MESH
MARGIN = 1.0
LOSS_SCALE = 128.0
D = 4096
SCALE = D ** (-0.5)
N_BLK = 128
NZ = 16
NXY = 8
PB = 128
QB = 512
HALF = 256
WIDTH = 1024

OWN, R, F, K, FR, KR, FAR = range(7)
OFFSET = {OWN: 0, R: 1, F: 2, K: -2, FR: 3, KR: -1, FAR: -3}
ROLES = (R, F, K, FR, KR, FAR)

ORDER = (
    "S0", "r0", "f0", "r1", "f1", "H0", "r2", "f2", "r3", "f3", "S1", "S2", "H1", "S3", "k0", "H2", "k1",
    "H3", "G1", "k2", "G2", "k3", "S5", "B", "G3", "S4", "H5", "D3", "H4", "D1", "S6", "G5", "H6",
    "G4", "D5", "D4", "D2", "L", "G6", "G0", "D6", "D0", "Q", "N", "M", "Z", "X",
)
FC = 4
VM1 = 60
VM2 = 62
FWD_RUNG = True
RET_RUNG = False
RC = 4
RL = 1


def kernel(
    hq_hbm, hp_hbm, gain_hbm, pos_hbm, tail_hbm,
    gq_hbm, gp_hbm, gg_ref, loss_ref,
    hq, gain_ref, pos_ref, tail_ref, hpt, q, p, sx, rx, hb, hr, gt, rpart, fpart, kpart, ret_out, ret_in, dq, dp, zbuf, xbuf, lbuf,
    local_sem, out_sem, fwd_send, fwd_recv, x1_send, x1_recv, x2_send, x2_recv,
    x3_send, x3_recv, ret_send, ret_recv, z_send, z_recv, xy_send, xy_recv, loss_send, loss_recv, known,
):
    b = lax.axis_index("blk")
    f = lax.axis_index("feat")
    h = lax.rem(b, 2)
    x = b // 32
    z = lax.rem(b, 32) // 2
    core = lax.rem(f, 2)
    sigma = 1 - 2 * h

    def block_at(role):
        return lax.rem(b + N_BLK + sigma * OFFSET[role], N_BLK)

    def dev(role):
        return (block_at(role), f)

    mate = (b, f + 1 - 2 * core)
    across = (b, lax.rem(f + 2, 4))

    def z_peer(k):
        return (x * 32 + lax.rem(z + k, NZ) * 2 + h, f)

    place = x * 2 + h

    def xy_peer(k):
        e = lax.rem(place + k, NXY)
        return ((e // 2) * 32 + z * 2 + lax.rem(e, 2), f)

    load_hp = pltpu.make_async_copy(hp_hbm, hpt.at[OWN], local_sem.at[0])
    load_hq = pltpu.make_async_copy(hq_hbm, hq, local_sem.at[1])
    small = [
        pltpu.make_async_copy(src, dst, local_sem.at[2 + i])
        for i, (src, dst) in enumerate(
            ((gain_hbm, gain_ref), (pos_hbm, pos_ref), (tail_hbm, tail_ref))
        )
    ]
    for copy in [load_hp, load_hq] + small:
        copy.start()

    peers = [dev(r) for r in ROLES] + [mate, across]
    peers += [z_peer(k) for k in (1, 2, 3, NZ - 3, NZ - 2, NZ - 1)]
    peers += [xy_peer(k) for k in range(1, NXY)]
    barrier = pltpu.get_barrier_semaphore()
    for peer in peers:
        pl.semaphore_signal(barrier, inc=1, device_id=peer, device_id_type=MESH)
    pl.semaphore_wait(barrier, len(peers))

    def tell(i, steps):
        for side, k in enumerate((steps, NZ - steps)):
            pl.semaphore_signal(
                known.at[i, side], inc=1, device_id=z_peer(k), device_id_type=MESH
            )

    def heard(i):
        for side in range(2):
            pl.semaphore_wait(known.at[i, side], 1)

    tell(0, 3)

    def stage_b():
        heard(0)
        tell(1, 2)

    sends = []

    def send(src, dst, s_sem, r_sem, to):
        copy = pltpu.make_async_remote_copy(
            src_ref=src, dst_ref=dst, send_sem=s_sem, recv_sem=r_sem,
            device_id=to, device_id_type=MESH,
        )
        copy.start()
        sends.append(copy)
        return copy

    def forward(src, slot, i, to):
        rows = pl.ds(i * (PB // FC), PB // FC)
        return send(
            src.at[rows, :], hpt.at[slot, rows, :], fwd_send.at[slot, i], fwd_recv.at[slot, i], dev(to)
        )

    fwd = {}
    for i in range(FC):
        fwd[R, i] = forward(hp_hbm, R, i, R)
    for i in range(FC):
        fwd[K, i] = forward(hp_hbm, K, i, F)
        fwd[F, i] = forward(hp_hbm, F, i, K)

    for copy in small:
        copy.wait()
    gain = gain_ref[...]
    pos_rows = [pos_ref[pl.ds(i, 1), :] for i in range(4)]
    pos_all = jnp.concatenate(pos_rows, axis=1) - b * PB
    pos_half = (
        jnp.concatenate([pos_ref[pl.ds(2 * core, 1), :], pos_ref[pl.ds(2 * core + 1, 1), :]], axis=1)
        - b * PB
    )
    tail_half = jnp.concatenate(
        [tail_ref[pl.ds(2 * core, 1), :], tail_ref[pl.ds(2 * core + 1, 1), :]], axis=1
    )
    count_half = tail_half.astype(jnp.float32)
    col_half = lax.broadcasted_iota(jnp.int32, (PB, HALF), 0)

    x1, x2, x3, ret = {}, {}, {}, {}
    state = {"anchor": None, "loss": 0.0, "total": 0.0, "gain": 0.0}

    load_hq.wait()
    q[...] = (hq[...].astype(jnp.float32) * gain).astype(jnp.bfloat16)
    load_hp.wait()

    def relay_r(i):
        fwd[R, i].wait_recv()
        if not FWD_RUNG:
            fwd[KR, i] = forward(hpt.at[R], KR, i, F)
        fwd[FR, i] = forward(hpt.at[R], FR, i, K)

    def relay_f(i):
        fwd[F, i].wait_recv()
        if FWD_RUNG:
            fwd[KR, i] = forward(hpt.at[F], KR, i, R)

    def relay_k(i):
        fwd[KR, i].wait_recv()
        fwd[FAR, i] = forward(hpt.at[KR], FAR, i, F)

    def stage_s(t):
        if t in (K, FR, FAR):
            for i in range(FC):
                fwd[t, i].wait_recv()
        rows = pl.ds(t * PB, PB)
        tile = (hpt[t].astype(jnp.float32) * gain).astype(jnp.bfloat16)
        p[rows, :] = tile
        s = lax.dot_general(
            tile, q[...], (((1,), (1,)), ((), ())), preferred_element_type=jnp.float32
        ) * SCALE
        if t == OWN:
            hot = lax.broadcasted_iota(jnp.int32, (PB, QB), 0) == pos_all
            state["anchor"] = jnp.sum(jnp.where(hot, s, 0.0), axis=0, keepdims=True)
        s = s - state["anchor"]
        sx[t, 0] = s[:, :HALF]
        sx[t, 1] = s[:, HALF:]
        x1[t] = send(sx.at[t, 1 - core], rx.at[t], x1_send.at[t], x1_recv.at[t], mate)

    def stage_h(t):
        x1[t].wait_recv()
        hb[t] = (sx[t, core] + rx[t]).astype(jnp.bfloat16)
        x2[t] = send(hb.at[t], hr.at[t], x2_send.at[t], x2_recv.at[t], across)

    def stage_g(t):
        x2[t].wait_recv()
        excess = hb[t].astype(jnp.float32) + hr[t].astype(jnp.float32) + MARGIN
        signed = sigma * OFFSET[t]
        order = 2 * abs(OFFSET[t]) - jnp.where(signed > 0, 1, 0)
        live = order * PB + col_half < tail_half
        if t == OWN:
            hot = col_half == pos_half
            live = live & jnp.logical_not(hot)
        e = jnp.exp(-jnp.abs(excess))
        soft = jnp.maximum(excess, 0.0) + jnp.log1p(e)
        sig = jnp.where(excess >= 0.0, 1.0, e) / (1.0 + e)
        state["loss"] += jnp.sum(jnp.where(live, soft, 0.0), axis=0, keepdims=True)
        g = jnp.where(live, sig * (LOSS_SCALE / count_half), 0.0)
        state["total"] += jnp.sum(g, axis=0, keepdims=True)
        if t == OWN:
            g = g - jnp.where(hot, state["total"], 0.0)
            lbuf[core] = jnp.broadcast_to(state["loss"] / count_half, (8, HALF))
            state["lossx"] = send(
                lbuf.at[core], lbuf.at[core], loss_send.at[0], loss_recv.at[0], mate
            )
        rows = pl.ds(t * PB, PB)
        gt[core, rows, :] = g.astype(jnp.bfloat16)
        x3[t] = send(
            gt.at[core, rows, :], gt.at[core, rows, :], x3_send.at[t], x3_recv.at[t], mate
        )

    def give_rows(t, value, to, rows, i):
        slot = t - 1
        ret_out[slot, rows, :] = value.astype(jnp.bfloat16)
        ret[t, i] = send(
            ret_out.at[slot, rows, :], ret_in.at[slot, rows, :],
            ret_send.at[slot, i], ret_recv.at[slot, i], dev(to),
        )

    def give(t, value, to, chunks):
        n = PB // chunks
        for i in range(chunks):
            give_rows(t, value[i * n:(i + 1) * n], to, pl.ds(i * n, n), i)

    def add_on(t, part, after, to, chunks):
        n = PB // chunks
        for i in range(chunks):
            rows = pl.ds(i * n, n)
            value = part[rows, :]
            for other in after:
                ret[other, i].wait_recv()
                value = value + ret_in[other - 1, rows, :].astype(jnp.float32)
            give_rows(t, value, to, rows, i)

    def chain_l():
        if RET_RUNG:
            add_on(R, rpart, (FR,), R, RL)

    def chain_n():
        add_on(KR, kpart, (FAR,), R if RET_RUNG else K, RC)

    def chain_m():
        if RET_RUNG:
            add_on(F, fpart, (KR,), F, RC)
        else:
            add_on(R, rpart, (FR, KR), R, RC)

    pieces = {K: 1, F: RC if RET_RUNG else 1, FR: RL if RET_RUNG else RC, R: RL if RET_RUNG else RC}
    held = {R: rpart, F: fpart, KR: kpart} if RET_RUNG else {R: rpart, KR: kpart}

    def stage_d(t):
        x3[t].wait_recv()
        rows = pl.ds(t * PB, PB)
        part = jnp.dot(gt[0, rows, :], q[:HALF, :], preferred_element_type=jnp.float32)
        part = part + jnp.dot(gt[1, rows, :], q[HALF:, :], preferred_element_type=jnp.float32)
        part = part * SCALE
        if t == OWN:
            dp[...] = part
        elif t in held:
            held[t][...] = part
        elif t == FAR:
            give(t, part, K, RC)
        else:
            give(t, part, K if t == K else F, pieces[t])
        prod = part * hpt[t].astype(jnp.float32)
        state["gain"] += jnp.sum(prod.reshape(PB // 8, 8, WIDTH), axis=0)

    out_copies = []

    def stage_q():
        for i in range(2):
            rows = pl.ds(i * HALF, HALF)
            dquery = lax.dot_general(
                gt[i], p[...], (((0,), (0,)), ((), ())), preferred_element_type=jnp.float32
            ) * SCALE
            dq[rows, :] = dquery * gain
            copy = pltpu.make_async_copy(dq.at[rows, :], gq_hbm.at[rows, :], out_sem.at[i])
            copy.start()
            out_copies.append(copy)
            prod = dquery * hq[rows, :].astype(jnp.float32)
            state["gain"] += jnp.sum(prod.reshape(HALF // 8, 8, WIDTH), axis=0)
        vec = jnp.sum(state["gain"], axis=0, keepdims=True)
        for i in range(8):
            zbuf[z, pl.ds(i, 1), :] = vec[:, i * 128:(i + 1) * 128]
        heard(1)
        for k in range(1, NZ):
            z_copies.append(
                send(zbuf.at[z], zbuf.at[z], z_send.at[k - 1], z_recv.at[k - 1], z_peer(k))
            )

    z_copies, xy_copies = [], []

    def stage_z():
        for copy in z_copies:
            copy.wait_recv()
        line = zbuf[0]
        for i in range(1, NZ):
            line = line + zbuf[i]
        xbuf[place] = line
        for k in range(1, NXY):
            xy_copies.append(
                send(xbuf.at[place], xbuf.at[place], xy_send.at[k - 1], xy_recv.at[k - 1], xy_peer(k))
            )

    def stage_x():
        for copy in xy_copies:
            copy.wait_recv()
        plane = xbuf[0]
        for i in range(1, NXY):
            plane = plane + xbuf[i]
        gg_ref[...] = plane
        state["lossx"].wait_recv()
        loss_ref[...] = jnp.concatenate([lbuf[0, 0:1, :], lbuf[1, 0:1, :]], axis=1)

    stages = {
        "S": stage_s, "H": stage_h, "G": stage_g, "D": stage_d, "r": relay_r, "k": relay_k,
        "Q": stage_q, "Z": stage_z, "X": stage_x, "N": chain_n, "M": chain_m,
        "L": chain_l, "f": relay_f, "B": stage_b,
    }
    for step in ORDER:
        stages[step[0]](*[int(c) for c in step[1:]])

    total = dp[...]
    for t in (K, R, F):
        for i in range(pieces[t]):
            ret[t, i].wait_recv()
        total = total + ret_in[t - 1].astype(jnp.float32)
    dp[...] = total * gain
    copy = pltpu.make_async_copy(dp, gp_hbm, out_sem.at[2])
    copy.start()
    out_copies.append(copy)
    for copy in sends:
        copy.wait_send()
    for copy in out_copies:
        copy.wait()


def finish(*refs):
    sources, results, held, sem_in, sem_out = refs[:4], refs[4:8], refs[8:12], refs[12], refs[13]
    parts = [(i, slice(None)) for i in (1, 2, 3)]
    parts += [(0, pl.ds(j * (QB // 4), QB // 4)) for j in range(4)]
    copies = []
    for n, (i, rows) in enumerate(parts):
        into = pltpu.make_async_copy(sources[i].at[rows], held[i].at[rows], sem_in.at[n])
        out = pltpu.make_async_copy(held[i].at[rows], results[i].at[rows], sem_out.at[n])
        into.start()
        copies.append((into, out))
    for into, out in copies:
        into.wait()
        out.start()
    for _, out in copies:
        out.wait()


def shards(hidden_query, hidden_passage, embed_gain, positive, tail_count):
    vmem = pl.BlockSpec(memory_space=pltpu.VMEM)
    hbm = pl.BlockSpec(memory_space=pl.ANY)
    dma = pltpu.SemaphoreType.DMA
    gq, gp, gg, loss = pl.pallas_call(
        kernel,
        name="retrieval",
        out_shape=(
            jax.ShapeDtypeStruct((QB, WIDTH), jnp.float32),
            jax.ShapeDtypeStruct((PB, WIDTH), jnp.float32),
            jax.ShapeDtypeStruct((8, 128), jnp.float32),
            jax.ShapeDtypeStruct((1, QB), jnp.float32),
        ),
        in_specs=[hbm] * 5,
        out_specs=(hbm, hbm, vmem, vmem),
        scratch_shapes=[
            pltpu.VMEM((QB, WIDTH), jnp.bfloat16),
            pltpu.VMEM((1, WIDTH), jnp.float32),
            pltpu.VMEM((4, 128), jnp.int32),
            pltpu.VMEM((4, 128), jnp.int32),
            pltpu.VMEM((7, PB, WIDTH), jnp.bfloat16),
            pltpu.VMEM((QB, WIDTH), jnp.bfloat16),
            pltpu.VMEM((7 * PB, WIDTH), jnp.bfloat16),
            pltpu.VMEM((7, 2, PB, HALF), jnp.float32),
            pltpu.VMEM((7, PB, HALF), jnp.float32),
            pltpu.VMEM((7, PB, HALF), jnp.bfloat16),
            pltpu.VMEM((7, PB, HALF), jnp.bfloat16),
            pltpu.VMEM((2, 7 * PB, HALF), jnp.bfloat16),
            pltpu.VMEM((PB, WIDTH), jnp.float32),
            pltpu.VMEM((PB, WIDTH), jnp.float32),
            pltpu.VMEM((PB, WIDTH), jnp.float32),
            pltpu.VMEM((6, PB, WIDTH), jnp.bfloat16),
            pltpu.VMEM((6, PB, WIDTH), jnp.bfloat16),
            pltpu.VMEM((QB, WIDTH), jnp.float32),
            pltpu.VMEM((PB, WIDTH), jnp.float32),
            pltpu.VMEM((NZ, 8, 128), jnp.float32),
            pltpu.VMEM((NXY, 8, 128), jnp.float32),
            pltpu.VMEM((2, 8, HALF), jnp.float32),
            dma((5,)), dma((3,)), dma((7, FC)), dma((7, FC)), dma((7,)), dma((7,)), dma((7,)), dma((7,)),
            dma((7,)), dma((7,)), dma((6, RC)), dma((6, RC)), dma((NZ - 1,)), dma((NZ - 1,)),
            dma((NXY - 1,)), dma((NXY - 1,)), dma((1,)), dma((1,)),
            pltpu.SemaphoreType.REGULAR((2, 2)),
        ],
        compiler_params=pltpu.CompilerParams(
            collective_id=0, has_side_effects=True, vmem_limit_bytes=VM1 * 1024 * 1024
        ),
    )(
        hidden_query, hidden_passage, embed_gain.reshape(1, WIDTH),
        positive.reshape(4, 128), tail_count.reshape(4, 128),
    )
    outs = (gq, gp, gg, loss)
    gq, gp, gg, loss = pl.pallas_call(
        finish,
        name="finish",
        out_shape=tuple(jax.ShapeDtypeStruct(o.shape, o.dtype) for o in outs),
        in_specs=[hbm] * 4,
        out_specs=(hbm,) * 4,
        scratch_shapes=[pltpu.VMEM(o.shape, o.dtype) for o in outs] + [dma((7,)), dma((7,))],
        compiler_params=pltpu.CompilerParams(vmem_limit_bytes=VM2 * 1024 * 1024),
    )(*outs)
    return gq, gp, gg.reshape(WIDTH), loss.reshape(QB)


def solution(mesh):
    in_specs = (P("blk", "feat"), P("blk", "feat"), P("feat"), P("blk"), P("blk"))
    out_specs = (P("blk", "feat"), P("blk", "feat"), P("feat"), P("blk"))
    return jax.shard_map(shards, mesh=mesh, in_specs=in_specs, out_specs=out_specs, check_vma=False)
```

```python
import jax
import jax.numpy as jnp
from jax import lax
from jax.experimental import pallas as pl
from jax.experimental.pallas import tpu as pltpu
from jax.sharding import PartitionSpec as P

MESH = pl.DeviceIdType.MESH
MARGIN = 1.0
LOSS_SCALE = 128.0
D = 4096
SCALE = D ** (-0.5)
N_BLK = 128
NZ = 16
NXY = 8
PB = 128
QB = 512
HALF = 256
WIDTH = 1024

OWN, R, F, K, FR, KR, FAR = range(7)
OFFSET = {OWN: 0, R: 1, F: 2, K: -2, FR: 3, KR: -1, FAR: -3}
ROLES = (R, F, K, FR, KR, FAR)

ORDER = (
    "S0", "r0", "f0", "r1", "f1", "H0", "r2", "f2", "r3", "f3", "S1", "S2", "H1", "S3", "k0", "H2", "k1",
    "H3", "G1", "k2", "G2", "k3", "S5", "B", "G3", "S4", "H5", "D3", "H4", "D1", "S6", "G5", "H6",
    "G4", "D5", "D4", "D2", "L", "G6", "G0", "D6", "D0", "Q", "N", "M", "Z", "X",
)
FC = 4
VM1 = 60
VM2 = 62
FWD_RUNG = True
RET_RUNG = False
RC = 4
RL = 1


def kernel(
    hq_hbm, hp_hbm, gain_hbm, pos_hbm, tail_hbm,
    gq_hbm, gp_hbm, gg_ref, loss_ref,
    hq, gain_ref, pos_ref, tail_ref, hpt, q, p, sx, rx, hb, hr, gt, rpart, fpart, kpart, ret_out, ret_in, dq, dp, zbuf, xbuf, lbuf,
    local_sem, out_sem, fwd_send, fwd_recv, x1_send, x1_recv, x2_send, x2_recv,
    x3_send, x3_recv, ret_send, ret_recv, z_send, z_recv, xy_send, xy_recv, loss_send, loss_recv, known,
):
    b = lax.axis_index("blk")
    f = lax.axis_index("feat")
    h = lax.rem(b, 2)
    x = b // 32
    z = lax.rem(b, 32) // 2
    core = lax.rem(f, 2)
    sigma = 1 - 2 * h

    def block_at(role):
        return lax.rem(b + N_BLK + sigma * OFFSET[role], N_BLK)

    def dev(role):
        return (block_at(role), f)

    mate = (b, f + 1 - 2 * core)
    across = (b, lax.rem(f + 2, 4))

    def z_peer(k):
        return (x * 32 + lax.rem(z + k, NZ) * 2 + h, f)

    place = x * 2 + h

    def xy_peer(k):
        e = lax.rem(place + k, NXY)
        return ((e // 2) * 32 + z * 2 + lax.rem(e, 2), f)

    load_hp = pltpu.make_async_copy(hp_hbm, hpt.at[OWN], local_sem.at[0])
    load_hq = pltpu.make_async_copy(hq_hbm, hq, local_sem.at[1])
    small = [
        pltpu.make_async_copy(src, dst, local_sem.at[2 + i])
        for i, (src, dst) in enumerate(
            ((gain_hbm, gain_ref), (pos_hbm, pos_ref), (tail_hbm, tail_ref))
        )
    ]
    for copy in [load_hp, load_hq] + small:
        copy.start()

    peers = [dev(r) for r in ROLES] + [mate, across]
    peers += [z_peer(k) for k in (1, 2, 3, NZ - 3, NZ - 2, NZ - 1)]
    peers += [xy_peer(k) for k in range(1, NXY)]
    barrier = pltpu.get_barrier_semaphore()
    for peer in peers:
        pl.semaphore_signal(barrier, inc=1, device_id=peer, device_id_type=MESH)
    pl.semaphore_wait(barrier, len(peers))

    def tell(i, steps):
        for side, k in enumerate((steps, NZ - steps)):
            pl.semaphore_signal(
                known.at[i, side], inc=1, device_id=z_peer(k), device_id_type=MESH
            )

    def heard(i):
        for side in range(2):
            pl.semaphore_wait(known.at[i, side], 1)

    tell(0, 3)

    def stage_b():
        heard(0)
        tell(1, 2)

    sends = []

    def send(src, dst, s_sem, r_sem, to):
        copy = pltpu.make_async_remote_copy(
            src_ref=src, dst_ref=dst, send_sem=s_sem, recv_sem=r_sem,
            device_id=to, device_id_type=MESH,
        )
        copy.start()
        sends.append(copy)
        return copy

    def forward(src, slot, i, to):
        rows = pl.ds(i * (PB // FC), PB // FC)
        return send(
            src.at[rows, :], hpt.at[slot, rows, :], fwd_send.at[slot, i], fwd_recv.at[slot, i], dev(to)
        )

    fwd = {}
    for i in range(FC):
        fwd[R, i] = forward(hp_hbm, R, i, R)
        fwd[K, i] = forward(hp_hbm, K, i, F)
        fwd[F, i] = forward(hp_hbm, F, i, K)

    for copy in small:
        copy.wait()
    gain = gain_ref[...]
    pos_rows = [pos_ref[pl.ds(i, 1), :] for i in range(4)]
    pos_all = jnp.concatenate(pos_rows, axis=1) - b * PB
    pos_half = (
        jnp.concatenate([pos_ref[pl.ds(2 * core, 1), :], pos_ref[pl.ds(2 * core + 1, 1), :]], axis=1)
        - b * PB
    )
    tail_half = jnp.concatenate(
        [tail_ref[pl.ds(2 * core, 1), :], tail_ref[pl.ds(2 * core + 1, 1), :]], axis=1
    )
    count_half = tail_half.astype(jnp.float32)
    col_half = lax.broadcasted_iota(jnp.int32, (PB, HALF), 0)

    x1, x2, x3, ret = {}, {}, {}, {}
    state = {"anchor": None, "loss": 0.0, "total": 0.0, "gain": 0.0}

    load_hq.wait()
    q[...] = (hq[...].astype(jnp.float32) * gain).astype(jnp.bfloat16)
    load_hp.wait()

    def relay_r(i):
        fwd[R, i].wait_recv()
        if not FWD_RUNG:
            fwd[KR, i] = forward(hpt.at[R], KR, i, F)
        fwd[FR, i] = forward(hpt.at[R], FR, i, K)

    def relay_f(i):
        fwd[F, i].wait_recv()
        if FWD_RUNG:
            fwd[KR, i] = forward(hpt.at[F], KR, i, R)

    def relay_k(i):
        fwd[KR, i].wait_recv()
        fwd[FAR, i] = forward(hpt.at[KR], FAR, i, F)

    def stage_s(t):
        if t in (K, FR, FAR):
            for i in range(FC):
                fwd[t, i].wait_recv()
        rows = pl.ds(t * PB, PB)
        tile = (hpt[t].astype(jnp.float32) * gain).astype(jnp.bfloat16)
        p[rows, :] = tile
        s = lax.dot_general(
            tile, q[...], (((1,), (1,)), ((), ())), preferred_element_type=jnp.float32
        ) * SCALE
        if t == OWN:
            hot = lax.broadcasted_iota(jnp.int32, (PB, QB), 0) == pos_all
            state["anchor"] = jnp.sum(jnp.where(hot, s, 0.0), axis=0, keepdims=True)
        s = s - state["anchor"]
        sx[t, 0] = s[:, :HALF]
        sx[t, 1] = s[:, HALF:]
        x1[t] = send(sx.at[t, 1 - core], rx.at[t], x1_send.at[t], x1_recv.at[t], mate)

    def stage_h(t):
        x1[t].wait_recv()
        hb[t] = (sx[t, core] + rx[t]).astype(jnp.bfloat16)
        x2[t] = send(hb.at[t], hr.at[t], x2_send.at[t], x2_recv.at[t], across)

    def stage_g(t):
        x2[t].wait_recv()
        excess = hb[t].astype(jnp.float32) + hr[t].astype(jnp.float32) + MARGIN
        signed = sigma * OFFSET[t]
        order = 2 * abs(OFFSET[t]) - jnp.where(signed > 0, 1, 0)
        live = order * PB + col_half < tail_half
        if t == OWN:
            hot = col_half == pos_half
            live = live & jnp.logical_not(hot)
        e = jnp.exp(-jnp.abs(excess))
        soft = jnp.maximum(excess, 0.0) + jnp.log1p(e)
        sig = jnp.where(excess >= 0.0, 1.0, e) / (1.0 + e)
        state["loss"] += jnp.sum(jnp.where(live, soft, 0.0), axis=0, keepdims=True)
        g = jnp.where(live, sig * (LOSS_SCALE / count_half), 0.0)
        state["total"] += jnp.sum(g, axis=0, keepdims=True)
        if t == OWN:
            g = g - jnp.where(hot, state["total"], 0.0)
            lbuf[core] = jnp.broadcast_to(state["loss"] / count_half, (8, HALF))
            state["lossx"] = send(
                lbuf.at[core], lbuf.at[core], loss_send.at[0], loss_recv.at[0], mate
            )
        rows = pl.ds(t * PB, PB)
        gt[core, rows, :] = g.astype(jnp.bfloat16)
        x3[t] = send(
            gt.at[core, rows, :], gt.at[core, rows, :], x3_send.at[t], x3_recv.at[t], mate
        )

    def give_rows(t, value, to, rows, i):
        slot = t - 1
        ret_out[slot, rows, :] = value.astype(jnp.bfloat16)
        ret[t, i] = send(
            ret_out.at[slot, rows, :], ret_in.at[slot, rows, :],
            ret_send.at[slot, i], ret_recv.at[slot, i], dev(to),
        )

    def give(t, value, to, chunks):
        n = PB // chunks
        for i in range(chunks):
            give_rows(t, value[i * n:(i + 1) * n], to, pl.ds(i * n, n), i)

    def add_on(t, part, after, to, chunks):
        n = PB // chunks
        for i in range(chunks):
            rows = pl.ds(i * n, n)
            value = part[rows, :]
            for other in after:
                ret[other, i].wait_recv()
                value = value + ret_in[other - 1, rows, :].astype(jnp.float32)
            give_rows(t, value, to, rows, i)

    def chain_l():
        if RET_RUNG:
            add_on(R, rpart, (FR,), R, RL)

    def chain_n():
        add_on(KR, kpart, (FAR,), R if RET_RUNG else K, RC)

    def chain_m():
        if RET_RUNG:
            add_on(F, fpart, (KR,), F, RC)
        else:
            add_on(R, rpart, (FR, KR), R, RC)

    pieces = {K: 1, F: RC if RET_RUNG else 1, FR: RL if RET_RUNG else RC, R: RL if RET_RUNG else RC}
    held = {R: rpart, F: fpart, KR: kpart} if RET_RUNG else {R: rpart, KR: kpart}

    def stage_d(t):
        x3[t].wait_recv()
        rows = pl.ds(t * PB, PB)
        part = jnp.dot(gt[0, rows, :], q[:HALF, :], preferred_element_type=jnp.float32)
        part = part + jnp.dot(gt[1, rows, :], q[HALF:, :], preferred_element_type=jnp.float32)
        part = part * SCALE
        if t == OWN:
            dp[...] = part
        elif t in held:
            held[t][...] = part
        elif t == FAR:
            give(t, part, K, RC)
        else:
            give(t, part, K if t == K else F, pieces[t])
        prod = part * hpt[t].astype(jnp.float32)
        state["gain"] += jnp.sum(prod.reshape(PB // 8, 8, WIDTH), axis=0)

    out_copies = []

    def stage_q():
        for i in range(2):
            rows = pl.ds(i * HALF, HALF)
            dquery = lax.dot_general(
                gt[i], p[...], (((0,), (0,)), ((), ())), preferred_element_type=jnp.float32
            ) * SCALE
            dq[rows, :] = dquery * gain
            copy = pltpu.make_async_copy(dq.at[rows, :], gq_hbm.at[rows, :], out_sem.at[i])
            copy.start()
            out_copies.append(copy)
            prod = dquery * hq[rows, :].astype(jnp.float32)
            state["gain"] += jnp.sum(prod.reshape(HALF // 8, 8, WIDTH), axis=0)
        vec = jnp.sum(state["gain"], axis=0, keepdims=True)
        for i in range(8):
            zbuf[z, pl.ds(i, 1), :] = vec[:, i * 128:(i + 1) * 128]
        heard(1)
        for k in sorted(range(1, NZ), key=lambda k: abs(k - NZ // 2)):
            z_copies.append(
                send(zbuf.at[z], zbuf.at[z], z_send.at[k - 1], z_recv.at[k - 1], z_peer(k))
            )

    z_copies, xy_copies = [], []

    def stage_z():
        for copy in z_copies:
            copy.wait_recv()
        line = zbuf[0]
        for i in range(1, NZ):
            line = line + zbuf[i]
        xbuf[place] = line
        for k in range(1, NXY):
            xy_copies.append(
                send(xbuf.at[place], xbuf.at[place], xy_send.at[k - 1], xy_recv.at[k - 1], xy_peer(k))
            )

    def stage_x():
        for copy in xy_copies:
            copy.wait_recv()
        plane = xbuf[0]
        for i in range(1, NXY):
            plane = plane + xbuf[i]
        gg_ref[...] = plane
        state["lossx"].wait_recv()
        loss_ref[...] = jnp.concatenate([lbuf[0, 0:1, :], lbuf[1, 0:1, :]], axis=1)

    stages = {
        "S": stage_s, "H": stage_h, "G": stage_g, "D": stage_d, "r": relay_r, "k": relay_k,
        "Q": stage_q, "Z": stage_z, "X": stage_x, "N": chain_n, "M": chain_m,
        "L": chain_l, "f": relay_f, "B": stage_b,
    }
    for step in ORDER:
        stages[step[0]](*[int(c) for c in step[1:]])

    total = dp[...]
    for t in (K, R, F):
        for i in range(pieces[t]):
            ret[t, i].wait_recv()
        total = total + ret_in[t - 1].astype(jnp.float32)
    dp[...] = total * gain
    copy = pltpu.make_async_copy(dp, gp_hbm, out_sem.at[2])
    copy.start()
    out_copies.append(copy)
    for copy in sends:
        copy.wait_send()
    for copy in out_copies:
        copy.wait()


def finish(*refs):
    sources, results, held, sem_in, sem_out = refs[:4], refs[4:8], refs[8:12], refs[12], refs[13]
    parts = [(i, slice(None)) for i in (1, 2, 3)]
    parts += [(0, pl.ds(j * (QB // 4), QB // 4)) for j in range(4)]
    copies = []
    for n, (i, rows) in enumerate(parts):
        into = pltpu.make_async_copy(sources[i].at[rows], held[i].at[rows], sem_in.at[n])
        out = pltpu.make_async_copy(held[i].at[rows], results[i].at[rows], sem_out.at[n])
        into.start()
        copies.append((into, out))
    for into, out in copies:
        into.wait()
        out.start()
    for _, out in copies:
        out.wait()


def shards(hidden_query, hidden_passage, embed_gain, positive, tail_count):
    vmem = pl.BlockSpec(memory_space=pltpu.VMEM)
    hbm = pl.BlockSpec(memory_space=pl.ANY)
    dma = pltpu.SemaphoreType.DMA
    gq, gp, gg, loss = pl.pallas_call(
        kernel,
        name="retrieval",
        out_shape=(
            jax.ShapeDtypeStruct((QB, WIDTH), jnp.float32),
            jax.ShapeDtypeStruct((PB, WIDTH), jnp.float32),
            jax.ShapeDtypeStruct((8, 128), jnp.float32),
            jax.ShapeDtypeStruct((1, QB), jnp.float32),
        ),
        in_specs=[hbm] * 5,
        out_specs=(hbm, hbm, vmem, vmem),
        scratch_shapes=[
            pltpu.VMEM((QB, WIDTH), jnp.bfloat16),
            pltpu.VMEM((1, WIDTH), jnp.float32),
            pltpu.VMEM((4, 128), jnp.int32),
            pltpu.VMEM((4, 128), jnp.int32),
            pltpu.VMEM((7, PB, WIDTH), jnp.bfloat16),
            pltpu.VMEM((QB, WIDTH), jnp.bfloat16),
            pltpu.VMEM((7 * PB, WIDTH), jnp.bfloat16),
            pltpu.VMEM((7, 2, PB, HALF), jnp.float32),
            pltpu.VMEM((7, PB, HALF), jnp.float32),
            pltpu.VMEM((7, PB, HALF), jnp.bfloat16),
            pltpu.VMEM((7, PB, HALF), jnp.bfloat16),
            pltpu.VMEM((2, 7 * PB, HALF), jnp.bfloat16),
            pltpu.VMEM((PB, WIDTH), jnp.float32),
            pltpu.VMEM((PB, WIDTH), jnp.float32),
            pltpu.VMEM((PB, WIDTH), jnp.float32),
            pltpu.VMEM((6, PB, WIDTH), jnp.bfloat16),
            pltpu.VMEM((6, PB, WIDTH), jnp.bfloat16),
            pltpu.VMEM((QB, WIDTH), jnp.float32),
            pltpu.VMEM((PB, WIDTH), jnp.float32),
            pltpu.VMEM((NZ, 8, 128), jnp.float32),
            pltpu.VMEM((NXY, 8, 128), jnp.float32),
            pltpu.VMEM((2, 8, HALF), jnp.float32),
            dma((5,)), dma((3,)), dma((7, FC)), dma((7, FC)), dma((7,)), dma((7,)), dma((7,)), dma((7,)),
            dma((7,)), dma((7,)), dma((6, RC)), dma((6, RC)), dma((NZ - 1,)), dma((NZ - 1,)),
            dma((NXY - 1,)), dma((NXY - 1,)), dma((1,)), dma((1,)),
            pltpu.SemaphoreType.REGULAR((2, 2)),
        ],
        compiler_params=pltpu.CompilerParams(
            collective_id=0, has_side_effects=True, vmem_limit_bytes=VM1 * 1024 * 1024
        ),
    )(
        hidden_query, hidden_passage, embed_gain.reshape(1, WIDTH),
        positive.reshape(4, 128), tail_count.reshape(4, 128),
    )
    outs = (gq, gp, gg, loss)
    gq, gp, gg, loss = pl.pallas_call(
        finish,
        name="finish",
        out_shape=tuple(jax.ShapeDtypeStruct(o.shape, o.dtype) for o in outs),
        in_specs=[hbm] * 4,
        out_specs=(hbm,) * 4,
        scratch_shapes=[pltpu.VMEM(o.shape, o.dtype) for o in outs] + [dma((7,)), dma((7,))],
        compiler_params=pltpu.CompilerParams(vmem_limit_bytes=VM2 * 1024 * 1024),
    )(*outs)
    return gq, gp, gg.reshape(WIDTH), loss.reshape(QB)


def solution(mesh):
    in_specs = (P("blk", "feat"), P("blk", "feat"), P("feat"), P("blk"), P("blk"))
    out_specs = (P("blk", "feat"), P("blk", "feat"), P("feat"), P("blk"))
    return jax.shard_map(shards, mesh=mesh, in_specs=in_specs, out_specs=out_specs, check_vma=False)
```
